32 devices in a mesh: lat: 4 (over y, x), lon: 8 (over z, core).
Axes of the slice: x: 2, y: 2, z: 4, core: 2. Of those that a mesh axis runs over, the one named last changes fastest.
Arguments:
- features: bfloat16 [128, 192, 2048], P('lat', 'lon'), may hold values from -6 to 6
- atrous_weight: bfloat16 [3, 3, 2048, 256], replicated, may hold values from -0.046875 to 0.046875
- norm_gain: float32 [256], replicated, may hold values from 0.1 to 1.9
- norm_bias: float32 [256], replicated, may hold values from -0.5 to 0.5
- head_weight: float32 [3, 256], replicated, may hold values from -1.5 to 1.5
- labels: int32 [128, 192], P('lat', 'lon'), may hold values from 0 to 2
Outputs:
- mean_loss: float32 [], replicated
- grad_features: bfloat16 [128, 192, 2048], P('lat', 'lon')
- grad_weight: float32 [2048, 3, 3, 256], P('lat', None, None, 'lon')
- grad_gain: float32 [256], replicated
- grad_bias: float32 [256], replicated
- grad_head: float32 [3, 256], replicated
The draws below stay inside these ranges and needn't reach their ends.
All inputs are finite; a program needn't handle non-finite values.
Results may differ from the reference program's by a relative error of at most 0.022.
Values may be sent and summed in bfloat16 or wider, within the bound.
A program may use at most 192 MiB of HBM per device.

```python
import jax
import jax.numpy as jnp
from jax import lax

CIN = 2048
COUT = 256
CLASSES = 3
RATE = 12
H = 128
W = 192


def touch_ends(entries, key, smallest, high):
    extent = entries.shape
    spot = [jax.random.randint(jax.random.fold_in(key, axis), (), 0, extent[axis]) for axis in range(len(extent))]
    entries = entries.at[tuple(spot)].set(smallest)
    longest = extent.index(max(extent))
    spot[longest] = (spot[longest] + 1) % extent[longest]
    return entries.at[tuple(spot)].set(high)


def block_levels(rng, extent, cuts, least, high):
    level = 1.0
    for dim, parts in cuts:
        steps = jax.random.uniform(jax.random.fold_in(jax.random.fold_in(rng, 6), dim), (parts,), jnp.float32, least / len(cuts), high / len(cuts))
        level = level * jnp.repeat(jnp.exp(steps), extent[dim] // parts).reshape((-1,) + (1,) * (len(extent) - 1 - dim))
    return level


def bell_draw(own_key, extent, scale, bound, shards=(), kind=jnp.bfloat16):
    gain = block_levels(own_key, extent, shards, -0.22, 0.18) if shards else 1.0
    entries = jax.random.normal(own_key, extent, jnp.float32) * scale * gain
    return jnp.minimum(jnp.maximum(entries, -bound), bound).astype(kind)


def setup_inputs(seed: int = 0) -> dict:
    arg_keys = jax.random.split(jax.random.key(seed), 7)
    return {
        "features": bell_draw(arg_keys[0], (H, W, CIN), 1.0, 6.0, ((0, 4), (1, 8))),
        "atrous_weight": bell_draw(arg_keys[1], (3, 3, CIN, COUT), (9 * CIN) ** -0.5, 0.046875),
        "norm_gain": jnp.clip(1.0 + 0.18 * jax.random.normal(arg_keys[2], (COUT,), jnp.float32), 0.1, 1.9),
        "norm_bias": jnp.clip(jax.random.uniform(arg_keys[3], (COUT,), jnp.float32, -0.5, 0.5), -0.5, 0.5),
        "head_weight": bell_draw(arg_keys[4], (CLASSES, COUT), 0.25, 1.5, (), jnp.float32),
        "labels": touch_ends(jax.random.randint(arg_keys[5], (H, W), 0, CLASSES), jax.random.fold_in(arg_keys[5], 1), 0, CLASSES - 1).astype(jnp.int32),
    }


epsilon = 1e-05

def cycle_pad(field):
    lon_padded = jnp.concatenate([field[:, W - RATE:], field, field[:, :RATE]], axis=1)
    return jnp.pad(lon_padded, ((RATE, RATE), (0, 0), (0, 0)))

def tap_window(padded, tap_row, tap_col):
    return padded[tap_row * RATE:tap_row * RATE + H, tap_col * RATE:tap_col * RATE + W]

def reference(features, atrous_weight, norm_gain, norm_bias, head_weight, labels):
    total_cells = H * W
    padded = cycle_pad(features)
    summed = jnp.zeros((total_cells, COUT), jnp.float32)
    for tap_row in range(3):
        for tap_col in range(3):
            window = tap_window(padded, tap_row, tap_col).reshape(total_cells, CIN)
            summed = summed + jnp.dot(window, atrous_weight[tap_row, tap_col], preferred_element_type=jnp.float32)
    average = lax.optimization_barrier(jnp.sum(summed, 0)) / total_cells
    variance = lax.optimization_barrier(jnp.sum(summed * summed, 0)) / total_cells - average * average
    inverse = lax.rsqrt(variance + epsilon)
    normed = (summed - average) * inverse
    preact = norm_gain * normed + norm_bias
    hidden = jnp.maximum(preact, 0.0).astype(jnp.bfloat16)
    hidden_wide = hidden.astype(jnp.float32)
    logits = jnp.dot(hidden_wide, head_weight.T, precision=lax.Precision.HIGHEST)
    one_hot = (labels.reshape(total_cells)[:, None] == jnp.arange(CLASSES, dtype=jnp.int32)[None, :]).astype(jnp.float32)
    exponent = jnp.exp(logits)
    partition = lax.optimization_barrier(jnp.sum(exponent, 1, keepdims=True))
    mean_loss = jnp.sum(jnp.log(partition)[:, 0] - lax.optimization_barrier(jnp.sum(logits * one_hot, 1))) / total_cells
    grad_logits = exponent / partition - one_hot
    grad_head = jnp.dot(grad_logits.T, hidden_wide, precision=lax.Precision.HIGHEST) / total_cells
    d_hidden = jnp.dot(grad_logits, head_weight, precision=lax.Precision.HIGHEST)
    d_preact = jnp.where(preact > 0, d_hidden, 0.0)
    grad_bias = lax.optimization_barrier(jnp.sum(d_preact, 0)) / total_cells
    grad_gain = lax.optimization_barrier(jnp.sum(d_preact * normed, 0)) / total_cells
    d_summed = (norm_gain * inverse * (d_preact - grad_bias - normed * grad_gain)).astype(jnp.bfloat16)
    grad_padded = cycle_pad(d_summed.reshape(H, W, COUT))
    grad_acc = jnp.zeros((total_cells, CIN), jnp.float32)
    kernel_rows = []
    for tap_row in range(3):
        kernel_cols = []
        for tap_col in range(3):
            shifted = tap_window(grad_padded, 2 - tap_row, 2 - tap_col).reshape(total_cells, COUT)
            grad_acc = grad_acc + lax.dot_general(shifted, atrous_weight[tap_row, tap_col], (((1,), (1,)), ((), ())), preferred_element_type=jnp.float32)
            window = tap_window(padded, tap_row, tap_col).reshape(total_cells, CIN)
            kernel_cols.append(jnp.dot(window.T, d_summed, preferred_element_type=jnp.float32) / total_cells)
        kernel_rows.append(jnp.stack(kernel_cols, 1))
    grad_weight = jnp.stack(kernel_rows, 1)
    grad_features = grad_acc.astype(jnp.bfloat16).reshape(H, W, CIN)
    return (mean_loss, grad_features, grad_weight, grad_gain, grad_bias, grad_head)
```

```python
import functools

import jax
import jax.numpy as jnp
from jax import lax
from jax.experimental import pallas as pl
from jax.experimental.pallas import tpu as pltpu
from jax.sharding import PartitionSpec as P

RATE = 12
MESH = pl.DeviceIdType.MESH


epsilon = 1e-05


def conv_kernel(x_ref, w_ref, out_ref):
    tap = pl.program_id(0)
    height, breadth, channels = x_ref.shape
    filters = w_ref.shape[-1]

    @pl.when(tap == 0)
    def _():
        out_ref[...] = jnp.zeros_like(out_ref)

    term = jnp.dot(
        x_ref[...].reshape(height * breadth, channels),
        w_ref[0, 0],
        preferred_element_type=jnp.float32,
    ).reshape(height, breadth, filters)
    row_first = (2 - tap // 3) * RATE
    for tap_col in range(3):

        @pl.when(tap % 3 == tap_col)
        def _():
            spot = (pl.ds(row_first, height), pl.ds((2 - tap_col) * RATE, breadth), slice(None))
            out_ref[spot] = out_ref[spot] + term


def spread_conv(features, weight):
    height, breadth, channels = features.shape
    filters = weight.shape[3]
    shape = (height + 2 * RATE, breadth + 2 * RATE, filters)
    return pl.pallas_call(
        conv_kernel,
        grid=(9,),
        in_specs=[
            pl.BlockSpec((height, breadth, channels), lambda t: (0, 0, 0)),
            pl.BlockSpec((1, 1, channels, filters), lambda t: (t // 3, t % 3, 0, 0)),
        ],
        out_specs=pl.BlockSpec(shape, lambda t: (0, 0, 0)),
        out_shape=jax.ShapeDtypeStruct(shape, jnp.float32),
        compiler_params=pltpu.CompilerParams(vmem_limit_bytes=48 * 1024 * 1024),
        cost_estimate=pl.CostEstimate(
            flops=18 * height * breadth * channels * filters,
            bytes_accessed=18 * channels * filters,
            transcendentals=0,
        ),
    )(features, weight)


def total_kernel(sizes, x_ref, out_ref, slots_lon, slots_lat, send_lon, recv_lon, send_lat, recv_lat):
    here = {axis: lax.axis_index(axis) for axis in sizes}

    def peer(axis, offset):
        where = dict(here)
        where[axis] = lax.rem(here[axis] + offset, sizes[axis])
        return (where["lat"], where["lon"])

    barrier = pltpu.get_barrier_semaphore()
    for axis in sizes:
        for offset in range(1, sizes[axis]):
            pl.semaphore_signal(barrier, inc=1, device_id=peer(axis, offset), device_id_type=MESH)
    pl.semaphore_wait(barrier, sum(sizes.values()) - len(sizes))

    def stage(axis, slots, send, recv):
        me = here[axis]
        copies = []
        for offset in range(1, sizes[axis]):
            copy = pltpu.make_async_remote_copy(
                src_ref=slots.at[me],
                dst_ref=slots.at[me],
                send_sem=send.at[offset],
                recv_sem=recv.at[offset],
                device_id=peer(axis, offset),
                device_id_type=MESH,
            )
            copy.start()
            copies.append(copy)
        for copy in copies:
            copy.wait()
        total = slots[0]
        for index in range(1, sizes[axis]):
            total = total + slots[index]
        return total

    slots_lon[here["lon"]] = x_ref[...]
    slots_lat[here["lat"]] = stage("lon", slots_lon, send_lon, recv_lon)
    out_ref[...] = stage("lat", slots_lat, send_lat, recv_lat)


def all_total(x, ident):
    sizes = {"lat": lax.axis_size("lat"), "lon": lax.axis_size("lon")}
    return pl.pallas_call(
        functools.partial(total_kernel, sizes),
        out_shape=jax.ShapeDtypeStruct(x.shape, x.dtype),
        in_specs=[pl.BlockSpec(memory_space=pltpu.VMEM)],
        out_specs=pl.BlockSpec(memory_space=pltpu.VMEM),
        scratch_shapes=[
            pltpu.VMEM((sizes["lon"],) + x.shape, x.dtype),
            pltpu.VMEM((sizes["lat"],) + x.shape, x.dtype),
            pltpu.SemaphoreType.DMA((sizes["lon"],)),
            pltpu.SemaphoreType.DMA((sizes["lon"],)),
            pltpu.SemaphoreType.DMA((sizes["lat"],)),
            pltpu.SemaphoreType.DMA((sizes["lat"],)),
        ],
        compiler_params=pltpu.CompilerParams(collective_id=ident, has_side_effects=True),
    )(x)


def gather_kernel(count, x_ref, out_ref, own_sem, send, recv):
    me = lax.axis_index("lat")
    lon = lax.axis_index("lon")
    barrier = pltpu.get_barrier_semaphore()
    for offset in range(1, count):
        pl.semaphore_signal(
            barrier, inc=1, device_id=(lax.rem(me + offset, count), lon), device_id_type=MESH
        )
    pl.semaphore_wait(barrier, count - 1)
    own = pltpu.make_async_copy(x_ref, out_ref.at[me], own_sem)
    own.start()
    copies = []
    for offset in range(1, count):
        copy = pltpu.make_async_remote_copy(
            src_ref=x_ref,
            dst_ref=out_ref.at[me],
            send_sem=send.at[offset],
            recv_sem=recv.at[offset],
            device_id=(lax.rem(me + offset, count), lon),
            device_id_type=MESH,
        )
        copy.start()
        copies.append(copy)
    own.wait()
    for copy in copies:
        copy.wait()


def gather_lat(x, ident):
    count = lax.axis_size("lat")
    return pl.pallas_call(
        functools.partial(gather_kernel, count),
        out_shape=jax.ShapeDtypeStruct((count,) + x.shape, x.dtype),
        in_specs=[pl.BlockSpec(memory_space=pltpu.VMEM)],
        out_specs=pl.BlockSpec(memory_space=pltpu.VMEM),
        scratch_shapes=[
            pltpu.SemaphoreType.DMA,
            pltpu.SemaphoreType.DMA((count,)),
            pltpu.SemaphoreType.DMA((count,)),
        ],
        compiler_params=pltpu.CompilerParams(
            collective_id=ident, has_side_effects=True, vmem_limit_bytes=16 * 1024 * 1024
        ),
    )(x)


def ring(axis, step, periodic):
    count = lax.axis_size(axis)
    pairs = [(i, i + step) for i in range(count)]
    if periodic:
        return [(i, j % count) for i, j in pairs]
    return [(i, j) for i, j in pairs if 0 <= j < count]


def shards(features, atrous_weight, norm_gain, norm_bias, head_weight, labels):
    height, breadth, channels = features.shape
    filters = atrous_weight.shape[3]
    classes = head_weight.shape[0]
    lats, lons = lax.axis_size("lat"), lax.axis_size("lon")
    lat = lax.axis_index("lat")
    local_cells = height * breadth
    total_cells = local_cells * lats * lons
    channel_block = channels // lats
    filter_block = filters // lons
    flat_input = features.reshape(local_cells, channels)

    strip = jnp.zeros((lats, local_cells, channel_block), jnp.bfloat16)
    for offset in range(lats):
        target = lax.rem(lat + offset, lats)
        piece = lax.dynamic_slice_in_dim(flat_input, target * channel_block, channel_block, 1)
        if offset:
            piece = lax.ppermute(piece, "lat", ring("lat", offset, True))
        source = lax.rem(lat + lats - offset, lats)
        strip = lax.dynamic_update_slice(strip, piece[None], (source, 0, 0))
    strip = strip.reshape(lats * local_cells, channel_block)

    spread = spread_conv(features, atrous_weight)
    from_left = lax.ppermute(spread[:, breadth + RATE :], "lon", ring("lon", 1, True))
    from_right = lax.ppermute(spread[:, :RATE], "lon", ring("lon", -1, True))
    center = (
        spread[:, RATE : RATE + breadth]
        + jnp.pad(from_left, ((0, 0), (0, breadth - RATE), (0, 0)))
        + jnp.pad(from_right, ((0, 0), (breadth - RATE, 0), (0, 0)))
    )
    from_above = lax.ppermute(center[height + RATE :], "lat", ring("lat", 1, False))
    from_below = lax.ppermute(center[:RATE], "lat", ring("lat", -1, False))
    summed = (
        center[RATE : RATE + height]
        + jnp.pad(from_above, ((0, height - RATE), (0, 0), (0, 0)))
        + jnp.pad(from_below, ((height - RATE, 0), (0, 0), (0, 0)))
    ).reshape(local_cells, filters)

    moments = all_total(
        jnp.pad(jnp.stack([jnp.sum(summed, 0), jnp.sum(summed * summed, 0)]), ((0, 6), (0, 0))), 0
    )
    average = moments[0] / total_cells
    variance = moments[1] / total_cells - average * average
    inverse = lax.rsqrt(variance + epsilon)
    normed = (summed - average) * inverse
    preact = norm_gain * normed + norm_bias
    hidden = jnp.maximum(preact, 0.0).astype(jnp.bfloat16)
    hidden_wide = hidden.astype(jnp.float32)
    logits = jnp.dot(hidden_wide, head_weight.T, precision=lax.Precision.HIGHEST)
    one_hot = (
        labels.reshape(local_cells)[:, None] == jnp.arange(classes, dtype=jnp.int32)[None, :]
    ).astype(jnp.float32)
    exponent = jnp.exp(logits)
    partition = jnp.sum(exponent, 1, keepdims=True)
    loss_terms = jnp.sum(jnp.log(partition)[:, 0] - jnp.sum(logits * one_hot, 1))
    grad_logits = exponent / partition - one_hot
    head_term = jnp.dot(grad_logits.T, hidden_wide, precision=lax.Precision.HIGHEST)
    d_hidden = jnp.dot(grad_logits, head_weight, precision=lax.Precision.HIGHEST)
    d_preact = jnp.where(preact > 0, d_hidden, 0.0)
    totals = all_total(
        jnp.concatenate(
            [
                jnp.sum(d_preact, 0)[None],
                jnp.sum(d_preact * normed, 0)[None],
                jnp.broadcast_to(loss_terms, (1, filters)),
                head_term,
                jnp.zeros((-(3 + classes) % 8, filters), jnp.float32),
            ]
        ),
        1,
    ) / total_cells
    grad_bias = totals[0]
    grad_gain = totals[1]
    mean_loss = totals[2, 0]
    grad_head = totals[3 : 3 + classes]
    d_summed = (norm_gain * inverse * (d_preact - grad_bias - normed * grad_gain)).astype(
        jnp.bfloat16
    )

    column = gather_lat(d_summed, 2).reshape(lats * height, breadth, filters)
    edge_left = lax.ppermute(column[:, breadth - RATE :], "lon", ring("lon", 1, True))
    edge_right = lax.ppermute(column[:, :RATE], "lon", ring("lon", -1, True))
    padded = jnp.pad(
        jnp.concatenate([edge_left, column, edge_right], 1), ((RATE, RATE), (0, 0), (0, 0))
    )
    near = lax.dynamic_slice_in_dim(padded, lat * height, height + 2 * RATE, 0)

    shifted_taps = []
    for tap_row in range(3):
        for tap_col in range(3):
            row_first = (2 - tap_row) * RATE
            col_first = (2 - tap_col) * RATE
            shifted_taps.append(
                padded[
                    row_first : row_first + lats * height, col_first : col_first + breadth
                ].reshape(lats * local_cells, filters)
            )
    lon_summed = lax.psum_scatter(
        jnp.einsum(
            "tqf,qc->ftc", jnp.stack(shifted_taps, 0), strip, preferred_element_type=jnp.float32
        ).astype(jnp.bfloat16),
        "lon",
        scatter_dimension=0,
        tiled=True,
    )
    grad_weight = (
        jnp.transpose(lon_summed.astype(jnp.float32), (2, 1, 0)) / total_cells
    ).reshape(channel_block, 3, 3, filter_block)

    grad_acc = jnp.zeros((local_cells, channels), jnp.float32)
    for tap_row in range(3):
        for tap_col in range(3):
            row_first = (2 - tap_row) * RATE
            col_first = (2 - tap_col) * RATE
            grad_acc = grad_acc + lax.dot_general(
                near[row_first : row_first + height, col_first : col_first + breadth].reshape(
                    local_cells, filters
                ),
                atrous_weight[tap_row, tap_col],
                (((1,), (1,)), ((), ())),
                preferred_element_type=jnp.float32,
            )
    grad_features = grad_acc.astype(jnp.bfloat16).reshape(height, breadth, channels)
    return (mean_loss, grad_features, grad_weight, grad_gain, grad_bias, grad_head)


def solution(mesh):
    return jax.shard_map(
        shards,
        mesh=mesh,
        in_specs=(P("lat", "lon", None), P(), P(), P(), P(), P("lat", "lon")),
        out_specs=(P(), P("lat", "lon", None), P("lat", None, None, "lon"), P(), P(), P()),
        check_vma=False,
    )
```

```python
import functools

import jax
import jax.numpy as jnp
from jax import lax
from jax.experimental import pallas as pl
from jax.experimental.pallas import tpu as pltpu
from jax.sharding import PartitionSpec as P

RATE = 12
MESH = pl.DeviceIdType.MESH


epsilon = 1e-05


def conv_kernel(x_ref, w_ref, out_ref):
    tap = pl.program_id(0)
    height, breadth, channels = x_ref.shape
    filters = w_ref.shape[-1]

    @pl.when(tap == 0)
    def _():
        out_ref[...] = jnp.zeros_like(out_ref)

    term = jnp.dot(
        x_ref[...].reshape(height * breadth, channels),
        w_ref[0, 0],
        preferred_element_type=jnp.float32,
    ).reshape(height, breadth, filters)
    row_first = (2 - tap // 3) * RATE
    for tap_col in range(3):

        @pl.when(tap % 3 == tap_col)
        def _():
            spot = (pl.ds(row_first, height), pl.ds((2 - tap_col) * RATE, breadth), slice(None))
            out_ref[spot] = out_ref[spot] + term


def spread_conv(features, weight):
    height, breadth, channels = features.shape
    filters = weight.shape[3]
    shape = (height + 2 * RATE, breadth + 2 * RATE, filters)
    return pl.pallas_call(
        conv_kernel,
        grid=(9,),
        in_specs=[
            pl.BlockSpec((height, breadth, channels), lambda t: (0, 0, 0)),
            pl.BlockSpec((1, 1, channels, filters), lambda t: (t // 3, t % 3, 0, 0)),
        ],
        out_specs=pl.BlockSpec(shape, lambda t: (0, 0, 0)),
        out_shape=jax.ShapeDtypeStruct(shape, jnp.float32),
        compiler_params=pltpu.CompilerParams(vmem_limit_bytes=48 * 1024 * 1024),
        cost_estimate=pl.CostEstimate(
            flops=18 * height * breadth * channels * filters,
            bytes_accessed=18 * channels * filters,
            transcendentals=0,
        ),
    )(features, weight)


def total_kernel(sizes, x_ref, out_ref, slots_lon, slots_lat, send_lon, recv_lon, send_lat, recv_lat):
    here = {axis: lax.axis_index(axis) for axis in sizes}

    def peer(axis, offset):
        where = dict(here)
        where[axis] = lax.rem(here[axis] + offset, sizes[axis])
        return (where["lat"], where["lon"])

    barrier = pltpu.get_barrier_semaphore()
    for axis in sizes:
        for offset in range(1, sizes[axis]):
            pl.semaphore_signal(barrier, inc=1, device_id=peer(axis, offset), device_id_type=MESH)
    pl.semaphore_wait(barrier, sum(sizes.values()) - len(sizes))

    def stage(axis, slots, send, recv):
        me = here[axis]
        copies = []
        for offset in range(1, sizes[axis]):
            copy = pltpu.make_async_remote_copy(
                src_ref=slots.at[me],
                dst_ref=slots.at[me],
                send_sem=send.at[offset],
                recv_sem=recv.at[offset],
                device_id=peer(axis, offset),
                device_id_type=MESH,
            )
            copy.start()
            copies.append(copy)
        for copy in copies:
            copy.wait()
        total = slots[0]
        for index in range(1, sizes[axis]):
            total = total + slots[index]
        return total

    slots_lon[here["lon"]] = x_ref[...]
    slots_lat[here["lat"]] = stage("lon", slots_lon, send_lon, recv_lon)
    out_ref[...] = stage("lat", slots_lat, send_lat, recv_lat)


def all_total(x, ident):
    sizes = {"lat": lax.axis_size("lat"), "lon": lax.axis_size("lon")}
    return pl.pallas_call(
        functools.partial(total_kernel, sizes),
        out_shape=jax.ShapeDtypeStruct(x.shape, x.dtype),
        in_specs=[pl.BlockSpec(memory_space=pltpu.VMEM)],
        out_specs=pl.BlockSpec(memory_space=pltpu.VMEM),
        scratch_shapes=[
            pltpu.VMEM((sizes["lon"],) + x.shape, x.dtype),
            pltpu.VMEM((sizes["lat"],) + x.shape, x.dtype),
            pltpu.SemaphoreType.DMA((sizes["lon"],)),
            pltpu.SemaphoreType.DMA((sizes["lon"],)),
            pltpu.SemaphoreType.DMA((sizes["lat"],)),
            pltpu.SemaphoreType.DMA((sizes["lat"],)),
        ],
        compiler_params=pltpu.CompilerParams(collective_id=ident, has_side_effects=True),
    )(x)


def gather_kernel(count, d_ref, out_ref, own_sem, send, recv, west_send, west_recv, east_send, east_recv):
    lat, lon = lax.axis_index("lat"), lax.axis_index("lon")
    lons = lax.axis_size("lon")
    breadth = d_ref.shape[0]
    west, east = lax.rem(lon + lons - 1, lons), lax.rem(lon + 1, lons)
    targets = [(lax.rem(lat + offset, count), lon) for offset in range(1, count)]

    barrier = pltpu.get_barrier_semaphore()
    for target in targets + [(lat, west), (lat, east)]:
        pl.semaphore_signal(barrier, inc=1, device_id=target, device_id_type=MESH)
    pl.semaphore_wait(barrier, count + 1)

    tiles = []
    for offset, target in enumerate(targets, 1):
        copy = pltpu.make_async_remote_copy(
            src_ref=d_ref,
            dst_ref=out_ref.at[lat, pl.ds(RATE, breadth)],
            send_sem=send.at[offset],
            recv_sem=recv.at[offset],
            device_id=target,
            device_id_type=MESH,
        )
        copy.start()
        tiles.append(copy)
    own = pltpu.make_async_copy(d_ref, out_ref.at[lat, pl.ds(RATE, breadth)], own_sem)
    own.start()
    own.wait()

    edges = []
    for offset in range(count):
        if offset:
            tiles[offset - 1].wait_recv()
        source = lax.rem(lat + count - offset, count)
        to_west = pltpu.make_async_remote_copy(
            src_ref=out_ref.at[source, pl.ds(RATE, RATE)],
            dst_ref=out_ref.at[source, pl.ds(RATE + breadth, RATE)],
            send_sem=west_send.at[offset],
            recv_sem=west_recv.at[offset],
            device_id=(lat, west),
            device_id_type=MESH,
        )
        to_east = pltpu.make_async_remote_copy(
            src_ref=out_ref.at[source, pl.ds(breadth, RATE)],
            dst_ref=out_ref.at[source, pl.ds(0, RATE)],
            send_sem=east_send.at[offset],
            recv_sem=east_recv.at[offset],
            device_id=(lat, east),
            device_id_type=MESH,
        )
        to_west.start()
        to_east.start()
        edges += [to_west, to_east]
    for copy in tiles:
        copy.wait_send()
    for copy in edges:
        copy.wait()


def gather_lat(d, ident):
    count = lax.axis_size("lat")
    breadth, height, filters = d.shape
    return pl.pallas_call(
        functools.partial(gather_kernel, count),
        out_shape=jax.ShapeDtypeStruct((count, breadth + 2 * RATE, height, filters), d.dtype),
        in_specs=[pl.BlockSpec(memory_space=pltpu.VMEM)],
        out_specs=pl.BlockSpec(memory_space=pltpu.VMEM),
        scratch_shapes=[pltpu.SemaphoreType.DMA] + [pltpu.SemaphoreType.DMA((count,))] * 6,
        compiler_params=pltpu.CompilerParams(
            collective_id=ident, has_side_effects=True, vmem_limit_bytes=24 * 1024 * 1024
        ),
    )(d)


def place_kernel(count, *refs):
    out_ref, sems = refs[count], refs[count + 1]
    lat = lax.axis_index("lat")
    copies = [
        pltpu.make_async_copy(
            refs[offset], out_ref.at[lax.rem(lat + count - offset, count)], sems.at[offset]
        )
        for offset in range(count)
    ]
    for copy in copies:
        copy.start()
    for copy in copies:
        copy.wait()


def place(pieces):
    count = len(pieces)
    return pl.pallas_call(
        functools.partial(place_kernel, count),
        out_shape=jax.ShapeDtypeStruct((count,) + pieces[0].shape, pieces[0].dtype),
        in_specs=[pl.BlockSpec(memory_space=pl.ANY)] * count,
        out_specs=pl.BlockSpec(memory_space=pl.ANY),
        scratch_shapes=[pltpu.SemaphoreType.DMA((count,))],
    )(*pieces)


def back_kernel(s_ref, w_ref, out_ref):
    filters = w_ref.shape[-1]
    total = None
    for tap in range(9):
        term = lax.dot_general(
            s_ref[:, tap * filters : (tap + 1) * filters],
            w_ref[tap // 3, tap % 3],
            (((1,), (1,)), ((), ())),
            preferred_element_type=jnp.float32,
        )
        total = term if total is None else total + term
    out_ref[...] = total.astype(out_ref.dtype)


def back_conv(windows, weight):
    cells = windows.shape[0]
    channels, filters = weight.shape[2:]
    width = 256
    return pl.pallas_call(
        back_kernel,
        grid=(channels // width,),
        in_specs=[
            pl.BlockSpec((cells, 9 * filters), lambda n: (0, 0)),
            pl.BlockSpec((3, 3, width, filters), lambda n: (0, 0, n, 0)),
        ],
        out_specs=pl.BlockSpec((cells, width), lambda n: (0, n)),
        out_shape=jax.ShapeDtypeStruct((cells, channels), jnp.bfloat16),
        compiler_params=pltpu.CompilerParams(vmem_limit_bytes=40 * 1024 * 1024),
        cost_estimate=pl.CostEstimate(
            flops=18 * cells * channels * filters,
            bytes_accessed=18 * channels * filters + 2 * cells * (channels + 9 * filters),
            transcendentals=0,
        ),
    )(windows, weight)


def ring(axis, step, periodic):
    count = lax.axis_size(axis)
    pairs = [(i, i + step) for i in range(count)]
    if periodic:
        return [(i, j % count) for i, j in pairs]
    return [(i, j) for i, j in pairs if 0 <= j < count]


def shards(features, atrous_weight, norm_gain, norm_bias, head_weight, labels):
    height, breadth, channels = features.shape
    filters = atrous_weight.shape[3]
    classes = head_weight.shape[0]
    lats, lons = lax.axis_size("lat"), lax.axis_size("lon")
    lat = lax.axis_index("lat")
    local_cells = height * breadth
    total_cells = local_cells * lats * lons
    channel_block = channels // lats
    filter_block = filters // lons
    flat_input = features.reshape(local_cells, channels)

    pieces = []
    for offset in range(lats):
        target = lax.rem(lat + offset, lats)
        piece = lax.dynamic_slice_in_dim(flat_input, target * channel_block, channel_block, 1)
        if offset:
            piece = lax.ppermute(piece, "lat", ring("lat", offset, True))
        pieces.append(piece)

    spread = spread_conv(features, atrous_weight)
    from_left = lax.ppermute(spread[:, breadth + RATE :], "lon", ring("lon", 1, True))
    from_right = lax.ppermute(spread[:, :RATE], "lon", ring("lon", -1, True))
    center = (
        spread[:, RATE : RATE + breadth]
        + jnp.pad(from_left, ((0, 0), (0, breadth - RATE), (0, 0)))
        + jnp.pad(from_right, ((0, 0), (breadth - RATE, 0), (0, 0)))
    )
    center, *pieces = lax.optimization_barrier((center, *pieces))
    from_above = lax.ppermute(center[height + RATE :], "lat", ring("lat", 1, False))
    from_below = lax.ppermute(center[:RATE], "lat", ring("lat", -1, False))
    summed = (
        center[RATE : RATE + height]
        + jnp.pad(from_above, ((0, height - RATE), (0, 0), (0, 0)))
        + jnp.pad(from_below, ((height - RATE, 0), (0, 0), (0, 0)))
    ).reshape(local_cells, filters)

    moments = all_total(
        jnp.pad(jnp.stack([jnp.sum(summed, 0), jnp.sum(summed * summed, 0)]), ((0, 6), (0, 0))), 0
    )
    average = moments[0] / total_cells
    variance = moments[1] / total_cells - average * average
    inverse = lax.rsqrt(variance + epsilon)
    normed = (summed - average) * inverse
    preact = norm_gain * normed + norm_bias
    hidden = jnp.maximum(preact, 0.0).astype(jnp.bfloat16)
    hidden_wide = hidden.astype(jnp.float32)
    logits = jnp.dot(hidden_wide, head_weight.T, precision=lax.Precision.HIGHEST)
    one_hot = (
        labels.reshape(local_cells)[:, None] == jnp.arange(classes, dtype=jnp.int32)[None, :]
    ).astype(jnp.float32)
    exponent = jnp.exp(logits)
    partition = jnp.sum(exponent, 1, keepdims=True)
    loss_terms = jnp.sum(jnp.log(partition)[:, 0] - jnp.sum(logits * one_hot, 1))
    grad_logits = exponent / partition - one_hot
    head_term = jnp.dot(grad_logits.T, hidden_wide, precision=lax.Precision.HIGHEST)
    d_hidden = jnp.dot(grad_logits, head_weight, precision=lax.Precision.HIGHEST)
    d_preact = jnp.where(preact > 0, d_hidden, 0.0)
    totals = all_total(
        jnp.concatenate(
            [
                jnp.sum(d_preact, 0)[None],
                jnp.sum(d_preact * normed, 0)[None],
                jnp.broadcast_to(loss_terms, (1, filters)),
                head_term,
                jnp.zeros((-(3 + classes) % 8, filters), jnp.float32),
            ]
        ),
        1,
    ) / total_cells
    grad_bias = totals[0]
    grad_gain = totals[1]
    mean_loss = totals[2, 0]
    grad_head = totals[3 : 3 + classes]
    d_summed = (norm_gain * inverse * (d_preact - grad_bias - normed * grad_gain)).astype(
        jnp.bfloat16
    )

    tiles = gather_lat(
        jnp.transpose(d_summed.reshape(height, breadth, filters), (1, 0, 2)), 2
    )
    padded = jnp.pad(
        jnp.transpose(tiles, (0, 2, 1, 3)).reshape(lats * height, breadth + 2 * RATE, filters),
        ((RATE, RATE), (0, 0), (0, 0)),
    )
    strip = place(pieces).reshape(lats * local_cells, channel_block)
    near = lax.dynamic_slice_in_dim(padded, lat * height, height + 2 * RATE, 0)

    shifted_taps = []
    for tap_row in range(3):
        for tap_col in range(3):
            row_first = (2 - tap_row) * RATE
            col_first = (2 - tap_col) * RATE
            shifted_taps.append(
                padded[
                    row_first : row_first + lats * height, col_first : col_first + breadth
                ].reshape(lats * local_cells, filters)
            )
    lon_summed = lax.psum_scatter(
        jnp.einsum(
            "tqf,qc->ftc", jnp.stack(shifted_taps, 0), strip, preferred_element_type=jnp.float32
        ).astype(jnp.bfloat16),
        "lon",
        scatter_dimension=0,
        tiled=True,
    )
    grad_weight = (
        jnp.transpose(lon_summed.astype(jnp.float32), (2, 1, 0)) / total_cells
    ).reshape(channel_block, 3, 3, filter_block)

    near_taps = []
    for tap_row in range(3):
        for tap_col in range(3):
            row_first = (2 - tap_row) * RATE
            col_first = (2 - tap_col) * RATE
            near_taps.append(
                near[row_first : row_first + height, col_first : col_first + breadth].reshape(
                    local_cells, filters
                )
            )
    grad_features = back_conv(jnp.concatenate(near_taps, 1), atrous_weight).reshape(
        height, breadth, channels
    )
    return (mean_loss, grad_features, grad_weight, grad_gain, grad_bias, grad_head)


def solution(mesh):
    return jax.shard_map(
        shards,
        mesh=mesh,
        in_specs=(P("lat", "lon", None), P(), P(), P(), P(), P("lat", "lon")),
        out_specs=(P(), P("lat", "lon", None), P("lat", None, None, "lon"), P(), P(), P()),
        check_vma=False,
    )
```
